768 devices in a mesh: gr: 32 (over z_lo, x, core), gc: 24 (over y, z_hi).
Axes of the slice: x: 4, y: 8, z: 12 (z_hi: 3, z_lo: 4; z = z_hi * 4 + z_lo), core: 2. Of those that a mesh axis runs over, the one named last changes fastest.
Arguments:
- features: bfloat16 [98304, 256], P(('gr', 'gc')), may hold values from -6 to 6
- degrees: int32 [98304], P(('gr', 'gc')), may hold values from 4 to 32
- weight: bfloat16 [256, 256], replicated, may hold values from -0.375 to 0.375
- bias_term: float32 [256], replicated, may hold values from -3 to 3
- tile_weights: bfloat16 [32, 24, 128, 128, 128], P('gr', 'gc'), may hold values from 0 to 1, as said below
- tile_rows: int32 [32, 24, 128], P('gr', 'gc'), may hold values from 0 to 23
- tile_columns: int32 [32, 24, 128], P('gr', 'gc'), may hold values from 0 to 31
- tile_count: int32 [32, 24], P('gr', 'gc'), may hold values from 16 to 128, as said below
- cotangent: bfloat16 [98304, 256], P(('gr', 'gc')), may hold values from -6 to 6
Outputs:
- activations: bfloat16 [98304, 256], P(('gr', 'gc'))
- feature_grad: bfloat16 [98304, 256], P(('gr', 'gc'))
The draws below stay inside these ranges and needn't reach their ends.
Inputs may be any that keep to these rules, and one draw needn't show every extreme that they name: `tile_weights`: edge weights; a tile's block holds a minority of nonzero entries. `tile_count`: 128 divided by 1, 2, 4 or 8; the occupied slots are the first ones; 128 is reached by some pair in every draw. `tile_rows`: slots may share a position. `tile_columns`: slots may share a position.
All inputs are finite; a program needn't handle non-finite values.
Results may differ from the reference program's by a relative error of at most 0.033.
Values may be sent and summed in bfloat16 or wider, within the bound.
No kernel may reach another device: no remote copies, remote signals or barrier semaphores. Data moves between devices by JAX's collectives and lax.ppermute only.
A program may use at most 64 MiB of HBM per device.

```python
import jax
import jax.numpy as jnp
from jax import lax

F = 256
TILE = 128
ROWS_DEV = 128
TILES_DEV = 128
NODES = 98304
ROW_BLOCKS = 24
COL_BLOCKS = 32
N_GR = 32
N_GC = 24


def draw_tile_weights(key, part):
    key = jax.random.fold_in(key, 11)
    uniform_draw = jax.random.uniform(key, (N_GR, N_GC, TILES_DEV, TILE, TILE), jnp.float32)
    stretched = uniform_draw * 32.0
    values = stretched
    return jnp.where(stretched < 1.0, values, 0.0).astype(jnp.bfloat16)


def draw_tile_count(key, part):
    key = jax.random.fold_in(key, 23)
    shift_key, full_key = jax.random.split(key)
    shifts = jax.random.randint(shift_key, (N_GR * N_GC,), 0, 4, dtype=jnp.int32)
    counts = TILES_DEV // jnp.left_shift(jnp.ones_like(shifts), shifts)
    chosen = jax.random.randint(full_key, (), 0, N_GR * N_GC, dtype=jnp.int32)
    counts = counts.at[chosen].set(TILES_DEV)
    return counts.reshape(N_GR, N_GC).astype(jnp.int32)


def touch_ends(array, own_key, smallest, largest):
    longest = array.shape.index(max(array.shape))
    spots = []
    for shift in (0, 1):
        where = [jax.random.randint(jax.random.fold_in(own_key, axis), (), 0, length) for axis, length in enumerate(array.shape)]
        where[longest] = (where[longest] + shift) % array.shape[longest]
        spots.append(tuple(where))
    return array.at[spots[0]].set(smallest).at[spots[1]].set(largest)


def steps_of(key, dims, cuts, smallest, top_value):
    level, own = 1.0, jax.random.fold_in(key, 6)
    for position, shards_of in cuts:
        draws = jnp.exp(jax.random.uniform(jax.random.fold_in(own, position), (shards_of,), jnp.float32, smallest / len(cuts), top_value / len(cuts)))
        level = level * jnp.repeat(draws, dims[position] // shards_of).reshape([-1 if axis == position else 1 for axis in range(len(dims))])
    return level


def gaussian(key, extent, deviation, bound, pieces=(), held_as=jnp.bfloat16):
    values = jax.random.normal(key, extent, jnp.float32) * deviation
    if len(pieces) > 0:
        values = steps_of(key, extent, pieces, -0.22, 0.18) * values
    return jnp.clip(values, min=-bound, max=bound).astype(held_as)


def setup_inputs(seed: int = 0) -> dict:
    seeds = jax.random.split(jax.random.key(seed), 10)
    features = gaussian(seeds[0], (NODES, F), 1.0, 6.0, ((0, 768),))
    degrees = touch_ends(jax.random.randint(seeds[1], (NODES,), 4, 33), jax.random.fold_in(seeds[1], 1), 4, 32).astype(jnp.int32)
    weight = gaussian(seeds[2], (F, F), F ** -0.5, 0.375)
    bias_term = gaussian(seeds[3], (F,), 0.5, 3.0, (), jnp.float32)
    tile_weights = draw_tile_weights(jax.random.fold_in(seeds[9], 71), 0)
    tile_rows = touch_ends(jax.random.randint(seeds[5], (N_GR, N_GC, TILES_DEV), 0, ROW_BLOCKS), jax.random.fold_in(seeds[5], 1), 0, ROW_BLOCKS - 1).astype(jnp.int32)
    tile_columns = touch_ends(jax.random.randint(seeds[6], (N_GR, N_GC, TILES_DEV), 0, COL_BLOCKS), jax.random.fold_in(seeds[6], 1), 0, COL_BLOCKS - 1).astype(jnp.int32)
    tile_count = draw_tile_count(jax.random.fold_in(seeds[9], 71), 0)
    cotangent = gaussian(seeds[8], (NODES, F), 1.0, 6.0, ((0, 768),))
    return {"features": features, "degrees": degrees, "weight": weight, "bias_term": bias_term, "tile_weights": tile_weights, "tile_rows": tile_rows, "tile_columns": tile_columns, "tile_count": tile_count, "cotangent": cotangent}


def spread_tiles(tile_block, pick_ids, place_ids, sources, place_blocks, live_count, transposed):
    tile_edge = tile_block.shape[-1]
    feat_width = sources.shape[-1]
    blocks = sources.reshape(-1, tile_edge, feat_width)
    chosen = jnp.take(blocks, pick_ids, axis=0).astype(jnp.float32)
    weights_f = tile_block.astype(jnp.float32)
    if transposed:
        product = jnp.einsum('tik,tif->tkf', weights_f, chosen)
    else:
        product = jnp.einsum('tik,tkf->tif', weights_f, chosen)
    is_live = (jnp.arange(tile_block.shape[0], dtype=jnp.int32) < live_count).astype(jnp.float32)
    product = product * is_live[:, None, None]
    summed = jax.ops.segment_sum(product, place_ids, num_segments=place_blocks)
    return summed.reshape(-1, feat_width)

def reference(features, degrees, weight, bias_term, tile_weights, tile_rows, tile_columns, tile_count, cotangent):
    inv_root = lax.rsqrt(degrees.astype(jnp.float32))[:, None]
    hidden = jnp.dot(features, weight, preferred_element_type=jnp.float32)
    scaled = (hidden * inv_root).astype(jnp.bfloat16)
    by_shard = scaled.reshape(N_GR, N_GC, ROWS_DEV, F)

    def forward_group(row_group):

        def add_pair(summed, col_group):
            sources = by_shard[:, col_group].reshape(N_GR * ROWS_DEV, F)
            partial_value = spread_tiles(tile_weights[row_group, col_group], tile_columns[row_group, col_group], tile_rows[row_group, col_group], sources, ROW_BLOCKS, tile_count[row_group, col_group], False)
            rounded = lax.optimization_barrier(partial_value.astype(jnp.bfloat16)).astype(jnp.float32)
            return (summed + rounded, None)
        summed, _ = lax.scan(add_pair, jnp.zeros((N_GC * ROWS_DEV, F), jnp.float32), jnp.arange(N_GC, dtype=jnp.int32))
        return summed
    gathered = lax.map(forward_group, jnp.arange(N_GR, dtype=jnp.int32)).reshape(NODES, F)
    preact = inv_root * (gathered + scaled.astype(jnp.float32)) + bias_term[None, :]
    sigmoid_value = jax.nn.sigmoid(preact)
    activations = (preact * sigmoid_value).astype(jnp.bfloat16)
    slope_value = sigmoid_value * (1.0 + preact * (1.0 - sigmoid_value))
    upstream = (cotangent.astype(jnp.float32) * slope_value * inv_root).astype(jnp.bfloat16)
    up_groups = upstream.reshape(N_GR, N_GC * ROWS_DEV, F)

    def backward_group(col_group):

        def add_pair(summed, row_group):
            partial_value = spread_tiles(tile_weights[row_group, col_group], tile_rows[row_group, col_group], tile_columns[row_group, col_group], up_groups[row_group], COL_BLOCKS, tile_count[row_group, col_group], True)
            rounded = lax.optimization_barrier(partial_value.astype(jnp.bfloat16)).astype(jnp.float32)
            return (summed + rounded, None)
        summed, _ = lax.scan(add_pair, jnp.zeros((N_GR * ROWS_DEV, F), jnp.float32), jnp.arange(N_GR, dtype=jnp.int32))
        return summed
    returned = lax.map(backward_group, jnp.arange(N_GC, dtype=jnp.int32))
    returned = returned.reshape(N_GC, N_GR, ROWS_DEV, F).transpose(1, 0, 2, 3).reshape(NODES, F)
    grad_hidden = (inv_root * (returned + upstream.astype(jnp.float32))).astype(jnp.bfloat16)
    feature_grad = jnp.einsum('nf,gf->ng', grad_hidden.astype(jnp.float32), weight.astype(jnp.float32))
    return (activations, feature_grad.astype(jnp.bfloat16))
```

```python
import functools

import jax
import jax.numpy as jnp
from jax import lax
from jax.experimental import pallas as pl
from jax.experimental.pallas import tpu as pltpu
from jax.sharding import Mesh
from jax.sharding import PartitionSpec as P

ZL, X, C, Y, ZH = 4, 4, 2, 8, 3
BF, F32 = jnp.bfloat16, jnp.float32
NODE_AXES = ("zl", "x", "c", "y", "zh")
UNROLL = 4


def accumulate(count_ref, pick_ref, place_ref, tiles_ref, src_ref, acc_ref, transposed):
    edge = tiles_ref.shape[-1]
    dims = (((0,), (0,)), ((), ())) if transposed else (((1,), (0,)), ((), ()))
    acc_ref[...] = jnp.zeros_like(acc_ref)

    def step(s, carry):
        products = []
        for u in range(UNROLL):
            t = s * UNROLL + u
            block = src_ref[pl.ds(pl.multiple_of(pick_ref[t] * edge, edge), edge), :]
            products.append(lax.dot_general(tiles_ref[t], block, dims, preferred_element_type=F32))
        for u in range(UNROLL):
            q = place_ref[s * UNROLL + u]
            acc_ref[pl.ds(pl.multiple_of(q * edge, edge), edge), :] += products[u]
        return carry

    lax.fori_loop(0, count_ref[0] // UNROLL, step, 0)


def forward_kernel(
    rows_a, count_ref, pick_ref, place_ref, tiles_ref, near_ref, far_ref, out_a, out_b, src, acc
):
    half = near_ref.shape[0]
    edge = tiles_ref.shape[-1]
    src[:half] = near_ref[...]
    src[half:] = far_ref[...]
    accumulate(count_ref, pick_ref, place_ref, tiles_ref, src, acc, False)
    for y in range(Y):
        for z in range(ZH):
            base = (y * ZH + z) * edge
            out_a[y, z] = acc[base : base + rows_a, :].astype(BF)
            out_b[z, y] = acc[base + rows_a : base + edge, :].astype(BF)


def backward_kernel(
    count_ref, pick_ref, place_ref, tiles_ref, part_a, part_b, near_ref, far_ref, src, acc
):
    edge = tiles_ref.shape[-1]
    rows_a = part_a.shape[2]
    for y in range(Y):
        for z in range(ZH):
            base = (y * ZH + z) * edge
            src[base : base + rows_a, :] = part_a[y, z]
            src[base + rows_a : base + edge, :] = part_b[z, y]
    accumulate(count_ref, pick_ref, place_ref, tiles_ref, src, acc, True)
    half = near_ref.shape[0]
    near_ref[...] = acc[:half, :].astype(BF)
    far_ref[...] = acc[half:, :].astype(BF)


SMEM = pl.BlockSpec(memory_space=pltpu.SMEM)
VMEM = pl.BlockSpec(memory_space=pltpu.VMEM)


def call(kernel, outs, src_rows, acc_rows, feat, *args):
    return pl.pallas_call(
        kernel,
        out_shape=tuple(jax.ShapeDtypeStruct(s, BF) for s in outs),
        in_specs=[SMEM] * 3 + [VMEM] * (len(args) - 3),
        out_specs=tuple(VMEM for _ in outs),
        scratch_shapes=[pltpu.VMEM((src_rows, feat), BF), pltpu.VMEM((acc_rows, feat), F32)],
        compiler_params=pltpu.CompilerParams(vmem_limit_bytes=40 * 1024 * 1024),
    )(*args)


def shift(n, k):
    return [(i, (i + k) % n) for i in range(n)]


def swap(value, axis):
    return lax.all_to_all(value, axis, 0, 0, tiled=True)


def spread(value, axis, size):
    return swap(jnp.broadcast_to(value[None], (size,) + value.shape), axis)


def total(value):
    return value.astype(F32).sum(0)


def body(
    features, degrees, weight, bias_term, tile_weights, tile_rows, tile_columns, tile_count, cotangent
):
    tiles = tile_weights[0, 0]
    rows, columns = tile_rows[0, 0], tile_columns[0, 0]
    count = tile_count[0]
    n, feat = features.shape
    my_x, my_c = lax.axis_index("x"), lax.axis_index("c")
    block_zl, block_x, block_c = columns // (X * C), columns // C % X, columns % C
    column_at = (block_c != my_c) * (X * ZL) + (my_x - block_x + X) % X * ZL + block_zl
    column_at = column_at.astype(jnp.int32)
    inv_root = lax.rsqrt(degrees.astype(F32))[:, None]
    hidden = jnp.dot(features, weight, preferred_element_type=F32)
    scaled = (hidden * inv_root).astype(BF)

    along_z = lax.all_gather(scaled, "zl", axis=0, tiled=True)
    near = jnp.concatenate(
        [along_z] + [lax.ppermute(along_z, "x", shift(X, k)) for k in range(1, X)], 0
    )
    far = lax.ppermute(near, "c", shift(C, 1))

    rows_a = 80
    rows_b = n - rows_a
    part_a, part_b = call(
        functools.partial(forward_kernel, rows_a),
        [(Y, ZH, rows_a, feat), (ZH, Y, rows_b, feat)],
        C * X * ZL * n, Y * ZH * n, feat,
        count, column_at, rows, tiles, near, far,
    )
    got_a = total(swap(part_a, "y")).astype(BF)
    got_b = total(swap(part_b, "zh")).astype(BF)
    own_a = total(swap(got_a, "zh"))
    own_b = total(swap(got_b, "y"))
    own_rows = jnp.concatenate([own_a, own_b], 0)

    preact = inv_root * (own_rows + scaled.astype(F32)) + bias_term[None, :]
    sigmoid_value = jax.nn.sigmoid(preact)
    activations = (preact * sigmoid_value).astype(BF)
    slope_value = sigmoid_value * (1.0 + preact * (1.0 - sigmoid_value))
    upstream = (cotangent.astype(F32) * slope_value * inv_root).astype(BF)

    up_a, up_b = upstream[:rows_a], upstream[rows_a:]
    up_a = spread(spread(up_a, "zh", ZH), "y", Y)
    up_b = spread(spread(up_b, "y", Y), "zh", ZH)
    half = (X * ZL * n, feat)
    own_half, other_half = call(
        backward_kernel, [half, half], Y * ZH * n, C * X * ZL * n, feat,
        count, rows, column_at, tiles, up_a, up_b,
    )
    other_half = lax.ppermute(other_half, "c", shift(C, 1))
    both = (own_half.astype(F32) + other_half.astype(F32)).astype(BF).reshape(X, ZL * n, feat)
    along_x = both[0].astype(F32)
    for k in range(1, X):
        along_x += lax.ppermute(both[k], "x", shift(X, -k)).astype(F32)
    own_back = total(swap(along_x.astype(BF).reshape(ZL, n, feat), "zl"))
    grad_hidden = (inv_root * (own_back + upstream.astype(F32))).astype(BF)
    feature_grad = jnp.einsum("nf,gf->ng", grad_hidden, weight, preferred_element_type=F32)
    return activations, feature_grad.astype(BF)


def solution(mesh):
    fine = Mesh(mesh.devices.reshape(ZL, X, C, Y, ZH), NODE_AXES)
    gr, gc = ("zl", "x", "c"), ("y", "zh")
    nodes = P(NODE_AXES, None)

    return jax.shard_map(
        body,
        mesh=fine,
        in_specs=(
            nodes, P(NODE_AXES), P(), P(), P(gr, gc, None, None, None), P(gr, gc, None), P(gr, gc, None),
            P(gr, gc), nodes,
        ),
        out_specs=(nodes, nodes),
        check_vma=False,
    )
```

```python
import functools

import jax
import jax.numpy as jnp
from jax import lax
from jax.experimental import pallas as pl
from jax.experimental.pallas import tpu as pltpu
from jax.sharding import Mesh
from jax.sharding import PartitionSpec as P

ZL, X, C, Y, ZH = 4, 4, 2, 8, 3
BF, F32 = jnp.bfloat16, jnp.float32
NODE_AXES = ("zl", "x", "c", "y", "zh")
UNROLL = 4


def accumulate(count_ref, pick_ref, place_ref, tiles_ref, src_ref, acc_ref, transposed):
    edge = tiles_ref.shape[-1]
    dims = (((0,), (0,)), ((), ())) if transposed else (((1,), (0,)), ((), ()))
    acc_ref[...] = jnp.zeros_like(acc_ref)

    def step(s, carry):
        products = []
        for u in range(UNROLL):
            t = s * UNROLL + u
            block = src_ref[pl.ds(pl.multiple_of(pick_ref[t] * edge, edge), edge), :]
            products.append(lax.dot_general(tiles_ref[t], block, dims, preferred_element_type=F32))
        for u in range(UNROLL):
            q = place_ref[s * UNROLL + u]
            acc_ref[pl.ds(pl.multiple_of(q * edge, edge), edge), :] += products[u]
        return carry

    lax.fori_loop(0, count_ref[0] // UNROLL, step, 0)


def forward_kernel(
    rows_a, count_ref, pick_ref, place_ref, zh_ref, tiles_ref, near_ref, far_ref, out_a, *rest
):
    out_b, (src, acc) = rest[:ZH], rest[ZH:]
    half = near_ref.shape[0]
    edge = tiles_ref.shape[-1]
    src[:half] = near_ref[...]
    src[half:] = far_ref[...]
    accumulate(count_ref, pick_ref, place_ref, tiles_ref, src, acc, False)
    for y in range(Y):
        for k in range(ZH):
            base = pl.multiple_of((y * ZH + (zh_ref[0] + k) % ZH) * edge, edge)
            out_a[y, k] = acc[pl.ds(base, rows_a), :].astype(BF)
            out_b[k][y] = acc[pl.ds(base + rows_a, edge - rows_a), :].astype(BF)


def backward_kernel(count_ref, pick_ref, place_ref, zh_ref, tiles_ref, part_a, *rest):
    part_b, (near_ref, far_ref, src, acc) = rest[:ZH], rest[ZH:]
    edge = tiles_ref.shape[-1]
    rows_a = part_a.shape[2]
    for y in range(Y):
        for k in range(ZH):
            base = pl.multiple_of((y * ZH + (zh_ref[0] + ZH - k) % ZH) * edge, edge)
            src[pl.ds(base, rows_a), :] = part_a[y, k]
            src[pl.ds(base + rows_a, edge - rows_a), :] = part_b[k][y]
    accumulate(count_ref, pick_ref, place_ref, tiles_ref, src, acc, True)
    half = near_ref.shape[0]
    near_ref[...] = acc[:half, :].astype(BF)
    far_ref[...] = acc[half:, :].astype(BF)


SMEM = pl.BlockSpec(memory_space=pltpu.SMEM)
VMEM = pl.BlockSpec(memory_space=pltpu.VMEM)


def call(kernel, outs, src_rows, acc_rows, feat, *args):
    return pl.pallas_call(
        kernel,
        out_shape=tuple(jax.ShapeDtypeStruct(s, BF) for s in outs),
        in_specs=[SMEM] * 4 + [VMEM] * (len(args) - 4),
        out_specs=tuple(VMEM for _ in outs),
        scratch_shapes=[pltpu.VMEM((src_rows, feat), BF), pltpu.VMEM((acc_rows, feat), F32)],
        compiler_params=pltpu.CompilerParams(vmem_limit_bytes=40 * 1024 * 1024),
    )(*args)


def shift(n, k):
    return [(i, (i + k) % n) for i in range(n)]


def swap(value, axis):
    return lax.all_to_all(value, axis, 0, 0, tiled=True)


def spread(value, axis, size):
    return swap(jnp.broadcast_to(value[None], (size,) + value.shape), axis)


def collect(pieces):
    moved = [pieces[0]] + [lax.ppermute(pieces[k], "zh", shift(ZH, k)) for k in range(1, ZH)]
    return sum(piece.astype(F32) for piece in moved)


def share(value):
    return [value] + [lax.ppermute(value, "zh", shift(ZH, k)) for k in range(1, ZH)]


def total(value):
    return value.astype(F32).sum(0)


def body(
    features, degrees, weight, bias_term, tile_weights, tile_rows, tile_columns, tile_count, cotangent
):
    tiles = tile_weights[0, 0]
    rows, columns = tile_rows[0, 0], tile_columns[0, 0]
    count = tile_count[0]
    n, feat = features.shape
    my_x, my_c = lax.axis_index("x"), lax.axis_index("c")
    my_zh = lax.axis_index("zh").astype(jnp.int32)[None]
    block_zl, block_x, block_c = columns // (X * C), columns // C % X, columns % C
    other = (block_c != my_c).astype(jnp.int32) * (X * ZL)
    column_at = other + (my_x - block_x + X) % X * ZL + block_zl
    sum_at = other + block_x * ZL + block_zl
    inv_root = lax.rsqrt(degrees.astype(F32))[:, None]
    hidden = jnp.dot(features, weight, preferred_element_type=F32)
    scaled = (hidden * inv_root).astype(BF)

    along_z = lax.all_gather(scaled, "zl", axis=0, tiled=True)
    near = jnp.concatenate(
        [along_z] + [lax.ppermute(along_z, "x", shift(X, k)) for k in range(1, X)], 0
    )
    far = lax.ppermute(near, "c", shift(C, 1))

    rows_a = 80
    rows_b = n - rows_a
    part_a, *part_b = call(
        functools.partial(forward_kernel, rows_a),
        [(Y, ZH, rows_a, feat)] + [(Y, rows_b, feat)] * ZH,
        C * X * ZL * n, Y * ZH * n, feat,
        count, column_at, rows, my_zh, tiles, near, far,
    )
    got_b = collect(part_b).astype(BF)
    got_a = total(swap(part_a, "y")).astype(BF)
    own_a = collect([got_a[k] for k in range(ZH)])
    own_b = total(swap(got_b, "y"))
    own_rows = jnp.concatenate([own_a, own_b], 0)

    preact = inv_root * (own_rows + scaled.astype(F32)) + bias_term[None, :]
    sigmoid_value = jax.nn.sigmoid(preact)
    activations = (preact * sigmoid_value).astype(BF)
    slope_value = sigmoid_value * (1.0 + preact * (1.0 - sigmoid_value))
    upstream = (cotangent.astype(F32) * slope_value * inv_root).astype(BF)

    up_a, up_b = upstream[:rows_a], upstream[rows_a:]
    up_b = share(spread(up_b, "y", Y))
    up_a = spread(jnp.stack(share(up_a)), "y", Y)
    half = (X * ZL * n, feat)
    own_half, other_half = call(
        backward_kernel, [half, half], Y * ZH * n, C * X * ZL * n, feat,
        count, rows, sum_at, my_zh, tiles, up_a, *up_b,
    )
    other_half = lax.ppermute(other_half, "c", shift(C, 1))
    both = (own_half.astype(F32) + other_half.astype(F32)).astype(BF).reshape(X, ZL * n, feat)
    along_x = total(swap(both, "x")).astype(BF).reshape(ZL, n, feat)
    own_back = total(swap(along_x, "zl"))
    grad_hidden = (inv_root * (own_back + upstream.astype(F32))).astype(BF)
    feature_grad = jnp.einsum("nf,gf->ng", grad_hidden, weight, preferred_element_type=F32)
    return activations, feature_grad.astype(BF)


def solution(mesh):
    fine = Mesh(mesh.devices.reshape(ZL, X, C, Y, ZH), NODE_AXES)
    gr, gc = ("zl", "x", "c"), ("y", "zh")
    nodes = P(NODE_AXES, None)

    return jax.shard_map(
        body,
        mesh=fine,
        in_specs=(
            nodes, P(NODE_AXES), P(), P(), P(gr, gc, None, None, None), P(gr, gc, None), P(gr, gc, None),
            P(gr, gc), nodes,
        ),
        out_specs=(nodes, nodes),
        check_vma=False,
    )
```

```python
import functools

import jax
import jax.numpy as jnp
from jax import lax
from jax.experimental import pallas as pl
from jax.experimental.pallas import tpu as pltpu
from jax.sharding import Mesh
from jax.sharding import PartitionSpec as P

ZL, X, C, Y, ZH = 4, 4, 2, 8, 3
BF, F32 = jnp.bfloat16, jnp.float32
NODE_AXES = ("zl", "x", "c", "y", "zh")
UNROLL = 4
PARTS = 4


def fetch(tiles_ref, tiles, sems):
    size = tiles.shape[0] // PARTS
    copies = []
    for part in range(PARTS):
        slots = pl.ds(part * size, size)
        copies.append(pltpu.make_async_copy(tiles_ref.at[slots], tiles.at[slots], sems.at[part]))
        copies[-1].start()
    return copies


def accumulate(count_ref, pick_ref, place_ref, tiles, copies, src, acc, transposed):
    edge = tiles.shape[-1]
    size = tiles.shape[0] // PARTS
    dims = (((0,), (0,)), ((), ())) if transposed else (((1,), (0,)), ((), ()))
    acc[...] = jnp.zeros_like(acc)

    for part in range(PARTS):
        copies[part].wait()

        def step(s, carry, first=part * size):
            products = []
            for u in range(UNROLL):
                t = first + s * UNROLL + u
                block = src[pl.ds(pl.multiple_of(pick_ref[t] * edge, edge), edge), :]
                products.append(lax.dot_general(tiles[t], block, dims, preferred_element_type=F32))
            for u in range(UNROLL):
                q = place_ref[first + s * UNROLL + u]
                acc[pl.ds(pl.multiple_of(q * edge, edge), edge), :] += products[u]
            return carry

        live = jnp.clip(count_ref[0] - part * size, 0, size)
        lax.fori_loop(0, live // UNROLL, step, 0)


def forward_kernel(
    count_ref, pick_ref, place_ref, at_ref, tiles_ref, near_ref, far_ref, out, src, acc, tiles, sems
):
    copies = fetch(tiles_ref, tiles, sems)
    half = near_ref.shape[0]
    edge = tiles.shape[-1]
    src[:half] = near_ref[...]
    src[half:] = far_ref[...]
    accumulate(count_ref, pick_ref, place_ref, tiles, copies, src, acc, False)
    for y in range(Y):
        for k in range(ZH):
            base = pl.multiple_of((y * ZH + (at_ref[0] + k) % ZH) * edge, edge)
            out[y, k] = acc[pl.ds(base, edge), :].astype(BF)


def backward_kernel(count_ref, pick_ref, place_ref, at_ref, tiles_ref, *rest):
    same, (next_a, next_b, near_ref, far_ref, src, acc, tiles, sems) = rest[: Y // 2], rest[Y // 2 :]
    copies = fetch(tiles_ref, tiles, sems)
    edge = tiles.shape[-1]
    cut = edge // 2
    for j in range(Y // 2):
        for k in range(ZH):
            z = (at_ref[0] + ZH - k) % ZH
            base, base_a, base_b = [
                pl.multiple_of(((at_ref[1 + i] + Y - 2 * j) % Y * ZH + z) * edge, edge) for i in range(3)
            ]
            src[pl.ds(base, edge), :] = same[j][k]
            src[pl.ds(base_a, cut), :] = next_a[j, k]
            src[pl.ds(base_b + cut, cut), :] = next_b[j, k]
    accumulate(count_ref, pick_ref, place_ref, tiles, copies, src, acc, True)
    half = near_ref.shape[0]
    near_ref[...] = acc[:half, :].astype(BF)
    far_ref[...] = acc[half:, :].astype(BF)


SMEM = pl.BlockSpec(memory_space=pltpu.SMEM)
VMEM = pl.BlockSpec(memory_space=pltpu.VMEM)
HBM = pl.BlockSpec(memory_space=pltpu.HBM)


def call(kernel, outs, src_rows, acc_rows, feat, *args):
    tiles = args[4]
    return pl.pallas_call(
        kernel,
        out_shape=tuple(jax.ShapeDtypeStruct(s, BF) for s in outs),
        in_specs=[SMEM] * 4 + [HBM] + [VMEM] * (len(args) - 5),
        out_specs=tuple(VMEM for _ in outs),
        scratch_shapes=[
            pltpu.VMEM((src_rows, feat), BF),
            pltpu.VMEM((acc_rows, feat), F32),
            pltpu.VMEM(tiles.shape, BF),
            pltpu.SemaphoreType.DMA((PARTS,)),
        ],
        compiler_params=pltpu.CompilerParams(vmem_limit_bytes=40 * 1024 * 1024),
    )(*args)


def shift(n, k):
    return [(i, (i + k) % n) for i in range(n)]


def swap(value, axis):
    return lax.all_to_all(value, axis, 0, 0, tiled=True)


def spread(value, axis, size):
    return swap(jnp.broadcast_to(value[None], (size,) + value.shape), axis)


def collect(pieces):
    moved = [pieces[0]] + [lax.ppermute(pieces[k], "zh", shift(ZH, k)) for k in range(1, ZH)]
    return sum(piece.astype(F32) for piece in moved)


def share(value, axis, size, stride):
    return [value] + [lax.ppermute(value, axis, shift(size, k)) for k in range(stride, size, stride)]


def total(value):
    return value.astype(F32).sum(0)


def body(
    features, degrees, weight, bias_term, tile_weights, tile_rows, tile_columns, tile_count, cotangent
):
    tiles = tile_weights[0, 0]
    rows, columns = tile_rows[0, 0], tile_columns[0, 0]
    count = tile_count[0]
    n, feat = features.shape
    my_y = lax.axis_index("y").astype(jnp.int32)
    my_zh = lax.axis_index("zh").astype(jnp.int32)
    odd = my_y % 2
    at = jnp.stack([my_zh, my_y, my_y + 1 - 2 * odd, (my_y + Y - 1 + 2 * odd) % Y])
    block_zl, block_x, block_c = columns // (X * C), columns // C % X, columns % C
    other = (block_c != lax.axis_index("c")).astype(jnp.int32)
    column_at = (other * X + block_x) * ZL + block_zl
    inv_root = lax.rsqrt(degrees.astype(F32))[:, None]
    hidden = jnp.dot(features, weight, preferred_element_type=F32)
    scaled = (hidden * inv_root).astype(BF)

    near = spread(spread(scaled, "zl", ZL), "x", X).reshape(X * ZL * n, feat)
    far = lax.ppermute(near, "c", shift(C, 1))
    (part,) = call(
        forward_kernel, [(Y, ZH, n, feat)], C * X * ZL * n, Y * ZH * n, feat,
        count, column_at, rows, at, tiles, near, far,
    )
    along_y = total(swap(part, "y")).astype(BF)
    own_rows = collect([along_y[k] for k in range(ZH)])

    preact = inv_root * (own_rows + scaled.astype(F32)) + bias_term[None, :]
    sigmoid_value = jax.nn.sigmoid(preact)
    activations = (preact * sigmoid_value).astype(BF)
    slope_value = sigmoid_value * (1.0 + preact * (1.0 - sigmoid_value))
    upstream = (cotangent.astype(F32) * slope_value * inv_root).astype(BF)

    mine = jnp.stack(share(upstream, "zh", ZH, 1))
    same = share(mine, "y", Y, 2)
    gathered = jnp.stack(same)
    next_a = lax.ppermute(gathered[:, :, : n // 2], "y", [(i, i ^ 1) for i in range(Y)])
    next_b = lax.ppermute(
        gathered[:, :, n // 2 :], "y", [(i, (i + 1 if i % 2 else i - 1) % Y) for i in range(Y)]
    )
    half = (X * ZL * n, feat)
    own_half, other_half = call(
        backward_kernel, [half, half], Y * ZH * n, C * X * ZL * n, feat,
        count, rows, column_at, at, tiles, *same, next_a, next_b,
    )
    other_half = lax.ppermute(other_half, "c", shift(C, 1))
    both = (own_half.astype(F32) + other_half.astype(F32)).astype(BF).reshape(X, ZL * n, feat)
    along_x = total(swap(both, "x")).astype(BF).reshape(ZL, n, feat)
    own_back = total(swap(along_x, "zl"))
    grad_hidden = (inv_root * (own_back + upstream.astype(F32))).astype(BF)
    feature_grad = jnp.einsum("nf,gf->ng", grad_hidden, weight, preferred_element_type=F32)
    return activations, feature_grad.astype(BF)


def solution(mesh):
    fine = Mesh(mesh.devices.reshape(ZL, X, C, Y, ZH), NODE_AXES)
    gr, gc = ("zl", "x", "c"), ("y", "zh")
    nodes = P(NODE_AXES, None)

    return jax.shard_map(
        body,
        mesh=fine,
        in_specs=(
            nodes, P(NODE_AXES), P(), P(), P(gr, gc, None, None, None), P(gr, gc, None), P(gr, gc, None),
            P(gr, gc), nodes,
        ),
        out_specs=(nodes, nodes),
        check_vma=False,
    )
```

```python
import jax
import jax.numpy as jnp
from jax import lax
from jax.experimental import pallas as pl
from jax.experimental.pallas import tpu as pltpu
from jax.sharding import Mesh
from jax.sharding import PartitionSpec as P

ZL, X, C, Y, ZH = 4, 4, 2, 8, 3
BF, F32 = jnp.bfloat16, jnp.float32
NODE_AXES = ("zl", "x", "c", "y", "zh")
UNROLL = 16


def accumulate(count_ref, pick_ref, place_ref, tiles_ref, src, acc, transposed):
    edge = tiles_ref.shape[-1]
    dims = (((0,), (0,)), ((), ())) if transposed else (((1,), (0,)), ((), ()))
    acc[...] = jnp.zeros_like(acc)

    def step(s, carry):
        for u in range(UNROLL):
            t = s * UNROLL + u
            block = src[pl.ds(pl.multiple_of(pick_ref[t] * edge, edge), edge), :]
            product = lax.dot_general(tiles_ref[t], block, dims, preferred_element_type=F32)
            acc[pl.ds(pl.multiple_of(place_ref[t] * edge, edge), edge), :] += product
        return carry

    lax.fori_loop(0, count_ref[0] // UNROLL, step, 0)


def forward_kernel(count_ref, pick_ref, place_ref, zh_ref, tiles_ref, near_ref, far_ref, out, src, acc):
    half = near_ref.shape[0]
    edge = tiles_ref.shape[-1]
    src[:half] = near_ref[...]
    src[half:] = far_ref[...]
    accumulate(count_ref, pick_ref, place_ref, tiles_ref, src, acc, False)
    for y in range(Y):
        for k in range(ZH):
            base = pl.multiple_of((y * ZH + (zh_ref[0] + k) % ZH) * edge, edge)
            out[y, k] = acc[pl.ds(base, edge), :].astype(BF)


def backward_kernel(count_ref, pick_ref, place_ref, zh_ref, tiles_ref, ups_ref, near_ref, far_ref, src, acc):
    edge = tiles_ref.shape[-1]
    for y in range(Y):
        for k in range(ZH):
            base = pl.multiple_of((y * ZH + (zh_ref[0] + ZH - k) % ZH) * edge, edge)
            src[pl.ds(base, edge), :] = ups_ref[y, k]
    accumulate(count_ref, pick_ref, place_ref, tiles_ref, src, acc, True)
    half = near_ref.shape[0]
    near_ref[...] = acc[:half, :].astype(BF)
    far_ref[...] = acc[half:, :].astype(BF)


SMEM = pl.BlockSpec(memory_space=pltpu.SMEM)
VMEM = pl.BlockSpec(memory_space=pltpu.VMEM)


def call(kernel, outs, src_rows, acc_rows, *args):
    feat = outs[0][-1]
    return pl.pallas_call(
        kernel,
        out_shape=tuple(jax.ShapeDtypeStruct(s, BF) for s in outs),
        in_specs=[SMEM] * 4 + [VMEM] * (len(args) - 4),
        out_specs=tuple(VMEM for _ in outs),
        scratch_shapes=[pltpu.VMEM((src_rows, feat), BF), pltpu.VMEM((acc_rows, feat), F32)],
        compiler_params=pltpu.CompilerParams(vmem_limit_bytes=24 * 1024 * 1024),
    )(*args)


def shift(n, k):
    return [(i, (i + k) % n) for i in range(n)]


def swap(value, axis):
    return lax.all_to_all(value, axis, 0, 0, tiled=True)


def spread(value, axis, size):
    return swap(jnp.broadcast_to(value[None], (size,) + value.shape), axis)


def collect(pieces, axis, step):
    size = len(pieces)
    moved = [lax.ppermute(pieces[k], axis, shift(size, step * k)) for k in range(1, size)]
    return sum((piece.astype(F32) for piece in moved), pieces[0].astype(F32))


def share(value, axis, size):
    return [value] + [lax.ppermute(value, axis, shift(size, k)) for k in range(1, size)]


def total(value):
    return value.astype(F32).sum(0)


def body(
    features, degrees, weight, bias_term, tile_weights, tile_rows, tile_columns, tile_count, cotangent
):
    tiles = tile_weights[0, 0]
    rows, columns = tile_rows[0, 0], tile_columns[0, 0]
    count = tile_count[0]
    n, feat = features.shape
    wide = feat // 2
    parts = (slice(0, wide), slice(wide, feat))
    my_x = lax.axis_index("x").astype(jnp.int32)
    my_zh = lax.axis_index("zh").astype(jnp.int32)[None]
    block_zl, block_x, block_c = columns // (X * C), columns // C % X, columns % C
    other = (block_c != lax.axis_index("c")).astype(jnp.int32) * (X * ZL)
    fixed = other + block_x * ZL + block_zl
    moving = other + (my_x + X - block_x) % X * ZL + block_zl
    sources, targets, chip = C * X * ZL * n, Y * ZH * n, X * ZL * n

    inv_root = lax.rsqrt(degrees.astype(F32))[:, None]
    hidden = jnp.dot(features, weight, preferred_element_type=F32)
    scaled = (hidden * inv_root).astype(BF)

    def forward(near, at):
        far = lax.ppermute(near, "c", shift(C, 1))
        (out,) = call(
            forward_kernel, [(Y, ZH, n, wide)], sources, targets,
            count, at, rows, my_zh, tiles, near, far,
        )
        return out

    def middle(partial, part, cotangent, after):
        along_y = total(swap(partial, "y")).astype(BF)
        own_rows = collect([along_y[k] for k in range(ZH)], "zh", 1)
        own_rows, _ = lax.optimization_barrier((own_rows, after))
        preact = inv_root * (own_rows + scaled[:, part].astype(F32)) + bias_term[None, part]
        sigmoid_value = jax.nn.sigmoid(preact)
        activations = (preact * sigmoid_value).astype(BF)
        slope_value = sigmoid_value * (1.0 + preact * (1.0 - sigmoid_value))
        upstream = (cotangent[:, part].astype(F32) * slope_value * inv_root).astype(BF)
        return activations, upstream, jnp.stack(share(upstream, "zh", ZH))

    def backward(ups, at):
        own, others = call(
            backward_kernel, [(chip, wide)] * 2, targets, sources, count, rows, at, my_zh, tiles, ups
        )
        others = lax.ppermute(others, "c", shift(C, 1))
        return (own.astype(F32) + others.astype(F32)).astype(BF).reshape(X, ZL * n, wide)

    along_z = spread(scaled, "zl", ZL)
    along_z = [along_z[:, :, part].reshape(ZL * n, wide) for part in parts]
    partial_0 = forward(spread(along_z[0], "x", X).reshape(chip, wide), fixed)
    partial_0, along_z[1] = lax.optimization_barrier((partial_0, along_z[1]))
    partial_1 = forward(jnp.concatenate(share(along_z[1], "x", X), 0), moving)

    activations_0, upstream_0, along_0 = middle(partial_0, parts[0], cotangent, ())
    activations_1, upstream_1, along_1 = middle(partial_1, parts[1], cotangent, upstream_0)

    ups_0, along_1 = lax.optimization_barrier((spread(along_0, "y", Y), along_1))
    ups_1 = spread(along_1, "y", Y)
    sums = backward(ups_0, moving)
    back_0 = collect([sums[k] for k in range(X)], "x", -1).astype(BF)
    ups_1, back_0 = lax.optimization_barrier((ups_1, back_0))
    back_1 = total(swap(backward(ups_1, fixed), "x")).astype(BF)
    back = jnp.concatenate([back_0, back_1], 1).reshape(ZL, n, feat)
    own_back = total(swap(back, "zl"))
    upstream = jnp.concatenate([upstream_0, upstream_1], 1)
    grad_hidden = (inv_root * (own_back + upstream.astype(F32))).astype(BF)
    feature_grad = jnp.einsum("nf,gf->ng", grad_hidden, weight, preferred_element_type=F32)
    return jnp.concatenate([activations_0, activations_1], 1), feature_grad.astype(BF)


def solution(mesh):
    fine = Mesh(mesh.devices.reshape(ZL, X, C, Y, ZH), NODE_AXES)
    gr, gc = ("zl", "x", "c"), ("y", "zh")
    nodes = P(NODE_AXES, None)
    return jax.shard_map(
        body,
        mesh=fine,
        in_specs=(
            nodes, P(NODE_AXES), P(), P(), P(gr, gc, None, None, None), P(gr, gc, None), P(gr, gc, None),
            P(gr, gc), nodes,
        ),
        out_specs=(nodes, nodes),
        check_vma=False,
    )
```

```python
import jax
import jax.numpy as jnp
from jax import lax
from jax.experimental import pallas as pl
from jax.experimental.pallas import tpu as pltpu
from jax.sharding import Mesh
from jax.sharding import PartitionSpec as P

ZL, X, C, Y, ZH = 4, 4, 2, 8, 3
BF, F32 = jnp.bfloat16, jnp.float32
NODE_AXES = ("zl", "x", "c", "y", "zh")
UNROLL = 16
PARTS = 4


def fetch(tiles_ref, tiles, sems):
    size = tiles.shape[0] // PARTS
    copies = []
    for part in range(PARTS):
        slots = pl.ds(part * size, size)
        copies.append(pltpu.make_async_copy(tiles_ref.at[slots], tiles.at[slots], sems.at[part]))
        copies[-1].start()
    return copies


def accumulate(count_ref, pick_ref, place_ref, tiles, copies, src, acc, transposed):
    edge = tiles.shape[-1]
    size = tiles.shape[0] // PARTS
    dims = (((0,), (0,)), ((), ())) if transposed else (((1,), (0,)), ((), ()))
    acc[...] = jnp.zeros_like(acc)

    for part in range(PARTS):
        copies[part].wait()

        def step(s, carry, first=part * size):
            for u in range(UNROLL):
                t = first + s * UNROLL + u
                block = src[pl.ds(pl.multiple_of(pick_ref[t] * edge, edge), edge), :]
                product = lax.dot_general(tiles[t], block, dims, preferred_element_type=F32)
                acc[pl.ds(pl.multiple_of(place_ref[t] * edge, edge), edge), :] += product
            return carry

        live = jnp.clip(count_ref[0] - part * size, 0, size)
        lax.fori_loop(0, live // UNROLL, step, 0)


def forward_kernel(
    count_ref, pick_ref, place_ref, zh_ref, tiles_ref, near_ref, far_ref, out, src, acc, tiles, sems
):
    copies = fetch(tiles_ref, tiles, sems)
    half = near_ref.shape[0]
    edge = tiles.shape[-1]
    src[:half] = near_ref[...]
    src[half:] = far_ref[...]
    accumulate(count_ref, pick_ref, place_ref, tiles, copies, src, acc, False)
    for y in range(Y):
        for k in range(ZH):
            base = pl.multiple_of((y * ZH + (zh_ref[0] + k) % ZH) * edge, edge)
            out[y, k] = acc[pl.ds(base, edge), :].astype(BF)


def backward_kernel(
    count_ref, pick_ref, place_ref, zh_ref, tiles_ref, ups_ref, near_ref, far_ref, src, acc, tiles, sems
):
    copies = fetch(tiles_ref, tiles, sems)
    edge = tiles.shape[-1]
    for y in range(Y):
        for k in range(ZH):
            base = pl.multiple_of((y * ZH + (zh_ref[0] + k) % ZH) * edge, edge)
            src[pl.ds(base, edge), :] = ups_ref[y, k]
    accumulate(count_ref, pick_ref, place_ref, tiles, copies, src, acc, True)
    half = near_ref.shape[0]
    near_ref[...] = acc[:half, :].astype(BF)
    far_ref[...] = acc[half:, :].astype(BF)


SMEM = pl.BlockSpec(memory_space=pltpu.SMEM)
VMEM = pl.BlockSpec(memory_space=pltpu.VMEM)
HBM = pl.BlockSpec(memory_space=pltpu.HBM)


def call(kernel, outs, src_rows, acc_rows, *args):
    feat = outs[0][-1]
    tiles = args[4]
    return pl.pallas_call(
        kernel,
        out_shape=tuple(jax.ShapeDtypeStruct(s, BF) for s in outs),
        in_specs=[SMEM] * 4 + [HBM] + [VMEM] * (len(args) - 5),
        out_specs=tuple(VMEM for _ in outs),
        scratch_shapes=[
            pltpu.VMEM((src_rows, feat), BF),
            pltpu.VMEM((acc_rows, feat), F32),
            pltpu.VMEM(tiles.shape, BF),
            pltpu.SemaphoreType.DMA((PARTS,)),
        ],
        compiler_params=pltpu.CompilerParams(vmem_limit_bytes=40 * 1024 * 1024),
    )(*args)


def shift(n, k):
    return [(i, (i + k) % n) for i in range(n)]


def swap(value, axis):
    return lax.all_to_all(value, axis, 0, 0, tiled=True)


def spread(value, axis, size):
    return swap(jnp.broadcast_to(value[None], (size,) + value.shape), axis)


def share(value, axis, size):
    return [value] + [lax.ppermute(value, axis, shift(size, k)) for k in range(1, size)]


def total(value):
    return value.astype(F32).sum(0)


def body(
    features, degrees, weight, bias_term, tile_weights, tile_rows, tile_columns, tile_count, cotangent
):
    tiles = tile_weights[0, 0]
    rows, columns = tile_rows[0, 0], tile_columns[0, 0]
    count = tile_count[0]
    n, feat = features.shape
    my_zh = lax.axis_index("zh").astype(jnp.int32)[None]
    other = (columns % C != lax.axis_index("c")).astype(jnp.int32)
    column_at = other * (ZL * X) + columns // C
    sources, targets, chip = C * ZL * X * n, Y * ZH * n, ZL * X * n

    degree = degrees.astype(F32)[:, None]
    inv_root = lax.rsqrt(degree)
    hidden = jnp.dot(features, weight, preferred_element_type=F32)
    scaled = (hidden * inv_root).astype(BF)

    near = spread(scaled, ("zl", "x"), ZL * X).reshape(chip, feat)
    far = lax.ppermute(near, "c", shift(C, 1))
    (partial,) = call(
        forward_kernel, [(Y, ZH, n, feat)], sources, targets,
        count, column_at, rows, my_zh, tiles, near, far,
    )
    along_y = total(swap(partial, "y")).astype(BF)
    shared = share(along_y, "zh", ZH)
    own_rows = sum(
        jnp.concatenate([shared[j][(k + j) % ZH] for k in range(ZH)], 0).astype(F32) for j in range(ZH)
    )
    beside = jnp.concatenate([cotangent, scaled, jnp.broadcast_to(degree.astype(BF), (n, n))], 1)
    beside = share(beside, "zh", ZH)
    beside = jnp.concatenate([beside[-k % ZH] for k in range(ZH)], 0).astype(F32)
    cotangents, scales = beside[:, :feat], beside[:, feat : 2 * feat]
    roots = lax.rsqrt(beside[:, 2 * feat : 2 * feat + 1])

    preact = roots * (own_rows + scales) + bias_term[None, :]
    sigmoid_value = jax.nn.sigmoid(preact)
    activations = (preact * sigmoid_value)[:n].astype(BF)
    slope_value = sigmoid_value * (1.0 + preact * (1.0 - sigmoid_value))
    upstream = (cotangents * slope_value * roots).astype(BF)

    ups = spread(upstream.reshape(ZH, n, feat), "y", Y)
    own, others = call(
        backward_kernel, [(chip, feat)] * 2, targets, sources, count, rows, column_at, my_zh, tiles, ups
    )
    others = lax.ppermute(others, "c", shift(C, 1))
    back = (own.astype(F32) + others.astype(F32)).astype(BF).reshape(ZL * X, n, feat)
    own_back = total(swap(back, ("zl", "x")))
    grad_hidden = (inv_root * (own_back + upstream[:n].astype(F32))).astype(BF)
    feature_grad = jnp.einsum("nf,gf->ng", grad_hidden, weight, preferred_element_type=F32)
    return activations, feature_grad.astype(BF)


def solution(mesh):
    fine = Mesh(mesh.devices.reshape(ZL, X, C, Y, ZH), NODE_AXES)
    gr, gc = ("zl", "x", "c"), ("y", "zh")
    nodes = P(NODE_AXES, None)
    return jax.shard_map(
        body,
        mesh=fine,
        in_specs=(
            nodes, P(NODE_AXES), P(), P(), P(gr, gc, None, None, None), P(gr, gc, None), P(gr, gc, None),
            P(gr, gc), nodes,
        ),
        out_specs=(nodes, nodes),
        check_vma=False,
    )
```

```python
import jax
import jax.numpy as jnp
from jax import lax
from jax.experimental import pallas as pl
from jax.experimental.pallas import tpu as pltpu
from jax.sharding import Mesh
from jax.sharding import PartitionSpec as P

ZL, X, C, Y, ZH = 4, 4, 2, 8, 3
BF, F32 = jnp.bfloat16, jnp.float32
NODE_AXES = ("zl", "x", "c", "y", "zh")
UNROLL = 16


def accumulate(count_ref, pick_ref, place_ref, tiles_ref, src, acc, transposed):
    edge = tiles_ref.shape[-1]
    dims = (((0,), (0,)), ((), ())) if transposed else (((1,), (0,)), ((), ()))
    acc[...] = jnp.zeros_like(acc)

    def step(s, carry):
        for u in range(UNROLL):
            t = s * UNROLL + u
            block = src[pl.ds(pl.multiple_of(pick_ref[t] * edge, edge), edge), :]
            product = lax.dot_general(tiles_ref[t], block, dims, preferred_element_type=F32)
            acc[pl.ds(pl.multiple_of(place_ref[t] * edge, edge), edge), :] += product
        return carry

    lax.fori_loop(0, count_ref[0] // UNROLL, step, 0)


def forward_kernel(count_ref, pick_ref, place_ref, zh_ref, tiles_ref, near_ref, far_ref, out, src, acc):
    half = near_ref.shape[0]
    edge = tiles_ref.shape[-1]
    src[:half] = near_ref[...]
    src[half:] = far_ref[...]
    accumulate(count_ref, pick_ref, place_ref, tiles_ref, src, acc, False)
    for y in range(Y):
        for k in range(ZH):
            base = pl.multiple_of((y * ZH + (zh_ref[0] + k) % ZH) * edge, edge)
            out[y, k] = acc[pl.ds(base, edge), :].astype(BF)


def backward_kernel(count_ref, pick_ref, place_ref, zh_ref, tiles_ref, ups_ref, near_ref, far_ref, src, acc):
    edge = tiles_ref.shape[-1]
    for y in range(Y):
        for k in range(ZH):
            base = pl.multiple_of((y * ZH + (zh_ref[0] + k) % ZH) * edge, edge)
            src[pl.ds(base, edge), :] = ups_ref[y, k]
    accumulate(count_ref, pick_ref, place_ref, tiles_ref, src, acc, True)
    half = near_ref.shape[0]
    near_ref[...] = acc[:half, :].astype(BF)
    far_ref[...] = acc[half:, :].astype(BF)


def pack_kernel(along_y_ref, scaled_ref, cotangent_ref, degree_ref, out):
    n = scaled_ref.shape[0]
    for k in range(ZH):
        summed = along_y_ref[0, k].astype(F32)
        for y in range(1, Y):
            summed += along_y_ref[y, k].astype(F32)
        if k == 0:
            summed += scaled_ref[...].astype(F32)
        out[k * n : (k + 1) * n, :] = summed.astype(BF)
    out[ZH * n : (ZH + 1) * n, :] = cotangent_ref[...]
    out[(ZH + 1) * n :, :] = degree_ref[...]


def middle_kernel(own_ref, back_1_ref, back_2_ref, bias_ref, activations_ref, upstream_ref, copies_ref):
    shared = (own_ref, back_1_ref, back_2_ref)
    n, wide = activations_ref.shape
    for k in range(ZH):
        gathered = shared[0][k * n : (k + 1) * n, :].astype(F32)
        for j in range(1, ZH):
            first = (k + j) % ZH * n
            gathered += shared[j][first : first + n, :].astype(F32)
        beside = shared[-k % ZH]
        degree = beside[(ZH + 1) * n :, :].astype(F32)[:1]
        root = lax.rsqrt(jnp.broadcast_to(degree, (wide, n)).T)
        preact = root * gathered + bias_ref[...]
        sigmoid_value = jax.nn.sigmoid(preact)
        slope_value = sigmoid_value * (1.0 + preact * (1.0 - sigmoid_value))
        cotangents = beside[ZH * n : (ZH + 1) * n, :].astype(F32)
        upstream = (cotangents * slope_value * root).astype(BF)
        if k == 0:
            activations_ref[...] = (preact * sigmoid_value).astype(BF)
            upstream_ref[...] = upstream
        for y in range(Y):
            copies_ref[y, k] = upstream


SMEM = pl.BlockSpec(memory_space=pltpu.SMEM)
VMEM = pl.BlockSpec(memory_space=pltpu.VMEM)


def call(kernel, outs, src_rows, acc_rows, *args):
    feat = outs[0][-1]
    return pl.pallas_call(
        kernel,
        out_shape=tuple(jax.ShapeDtypeStruct(s, BF) for s in outs),
        in_specs=[SMEM] * 4 + [VMEM] * (len(args) - 4),
        out_specs=tuple(VMEM for _ in outs),
        scratch_shapes=[pltpu.VMEM((src_rows, feat), BF), pltpu.VMEM((acc_rows, feat), F32)],
        compiler_params=pltpu.CompilerParams(vmem_limit_bytes=24 * 1024 * 1024),
    )(*args)


def call_small(kernel, outs, *args):
    return pl.pallas_call(
        kernel,
        out_shape=tuple(jax.ShapeDtypeStruct(s, BF) for s in outs),
        in_specs=[VMEM] * len(args),
        out_specs=tuple(VMEM for _ in outs),
        compiler_params=pltpu.CompilerParams(vmem_limit_bytes=24 * 1024 * 1024),
    )(*args)


def shift(n, k):
    return [(i, (i + k) % n) for i in range(n)]


def swap(value, axis):
    return lax.all_to_all(value, axis, 0, 0, tiled=True)


def spread(value, axis, size):
    return swap(jnp.broadcast_to(value[None], (size,) + value.shape), axis)


def collect(pieces, axis):
    size = len(pieces)
    moved = [lax.ppermute(pieces[k], axis, shift(size, -k)) for k in range(1, size)]
    return sum((piece.astype(F32) for piece in moved), pieces[0].astype(F32))


def share(value, axis, size):
    return [value] + [lax.ppermute(value, axis, shift(size, k)) for k in range(1, size)]


def total(value):
    return value.astype(F32).sum(0)


def body(
    features, degrees, weight, bias_term, tile_weights, tile_rows, tile_columns, tile_count, cotangent
):
    tiles = tile_weights[0, 0]
    rows, columns = tile_rows[0, 0], tile_columns[0, 0]
    count = tile_count[0]
    n, feat = features.shape
    wide = feat // 2
    parts = (slice(0, wide), slice(wide, feat))
    my_x = lax.axis_index("x").astype(jnp.int32)
    my_zh = lax.axis_index("zh").astype(jnp.int32)[None]
    block_zl, block_x, block_c = columns // (X * C), columns // C % X, columns % C
    other = (block_c != lax.axis_index("c")).astype(jnp.int32) * (X * ZL)
    fixed = other + block_x * ZL + block_zl
    moving = other + (my_x + X - block_x) % X * ZL + block_zl
    sources, targets, chip = C * X * ZL * n, Y * ZH * n, X * ZL * n

    inv_root = lax.rsqrt(degrees.astype(F32))[:, None]
    hidden = jnp.dot(features, weight, preferred_element_type=F32)
    scaled = (hidden * inv_root).astype(BF)

    def forward(near, at):
        far = lax.ppermute(near, "c", shift(C, 1))
        (out,) = call(
            forward_kernel, [(Y, ZH, n, wide)], sources, targets,
            count, at, rows, my_zh, tiles, near, far,
        )
        return out

    degree_rows = jnp.pad(degrees.astype(BF)[None], ((0, 15), (0, 0)))

    def middle(partial, part, after):
        beside, _ = lax.optimization_barrier(((scaled[:, part], cotangent[:, part], degree_rows), after))
        (mine,) = call_small(pack_kernel, [((ZH + 1) * n + 16, wide)], swap(partial, "y"), *beside)
        shared = share(mine, "zh", ZH)
        return call_small(
            middle_kernel, [(n, wide), (n, wide), (Y, ZH, n, wide)], *shared, bias_term[None, part]
        )

    def backward(ups, at):
        own, others = call(
            backward_kernel, [(chip, wide)] * 2, targets, sources, count, rows, at, my_zh, tiles, ups
        )
        others = lax.ppermute(others, "c", shift(C, 1))
        return (own.astype(F32) + others.astype(F32)).astype(BF).reshape(X, ZL * n, wide)

    along_z = spread(scaled, "zl", ZL)
    along_z = [along_z[:, :, part].reshape(ZL * n, wide) for part in parts]
    partial_0 = forward(spread(along_z[0], "x", X).reshape(chip, wide), fixed)
    partial_0, along_z[1] = lax.optimization_barrier((partial_0, along_z[1]))
    partial_1 = forward(jnp.concatenate(share(along_z[1], "x", X), 0), moving)

    activations_0, upstream_0, along_0 = middle(partial_0, parts[0], ())
    activations_1, upstream_1, along_1 = middle(partial_1, parts[1], upstream_0)

    ups_0, along_1 = lax.optimization_barrier((swap(along_0, "y"), along_1))
    ups_1 = swap(along_1, "y")
    sums = backward(ups_0, moving)
    back_0 = collect([sums[k] for k in range(X)], "x").astype(BF)
    ups_1, back_0 = lax.optimization_barrier((ups_1, back_0))
    back_1 = total(swap(backward(ups_1, fixed), "x")).astype(BF)
    back = jnp.concatenate([back_0, back_1], 1).reshape(ZL, n, feat)
    own_back = total(swap(back, "zl"))
    upstream = jnp.concatenate([upstream_0, upstream_1], 1)
    grad_hidden = (inv_root * (own_back + upstream.astype(F32))).astype(BF)
    feature_grad = jnp.einsum("nf,gf->ng", grad_hidden, weight, preferred_element_type=F32)
    return jnp.concatenate([activations_0, activations_1], 1), feature_grad.astype(BF)


def solution(mesh):
    fine = Mesh(mesh.devices.reshape(ZL, X, C, Y, ZH), NODE_AXES)
    gr, gc = ("zl", "x", "c"), ("y", "zh")
    nodes = P(NODE_AXES, None)
    return jax.shard_map(
        body,
        mesh=fine,
        in_specs=(
            nodes, P(NODE_AXES), P(), P(), P(gr, gc, None, None, None), P(gr, gc, None), P(gr, gc, None),
            P(gr, gc), nodes,
        ),
        out_specs=(nodes, nodes),
        check_vma=False,
    )
```

```python
import functools

import jax
import jax.numpy as jnp
from jax import lax
from jax.experimental import pallas as pl
from jax.experimental.pallas import tpu as pltpu
from jax.sharding import Mesh
from jax.sharding import PartitionSpec as P

ZL, X, C, Y, ZH = 4, 4, 2, 8, 3
BF, F32 = jnp.bfloat16, jnp.float32
NODE_AXES = ("zl", "x", "c", "y", "zh")
UNROLL = 16


def accumulate(count_ref, pick_ref, place_ref, tiles_ref, src, acc, transposed):
    edge = tiles_ref.shape[-1]
    dims = (((0,), (0,)), ((), ())) if transposed else (((1,), (0,)), ((), ()))
    acc[...] = jnp.zeros_like(acc)

    def step(s, carry):
        for u in range(UNROLL):
            t = s * UNROLL + u
            block = src[pl.ds(pl.multiple_of(pick_ref[t] * edge, edge), edge), :]
            product = lax.dot_general(tiles_ref[t], block, dims, preferred_element_type=F32)
            acc[pl.ds(pl.multiple_of(place_ref[t] * edge, edge), edge), :] += product
        return carry

    lax.fori_loop(0, count_ref[0] // UNROLL, step, 0)


def forward_kernel(
    count_ref, pick_ref, place_ref, zh_ref, tiles_ref, near_ref, far_ref, out_0, out_1, src, acc
):
    half = near_ref.shape[0]
    edge = tiles_ref.shape[-1]
    wide = out_0.shape[-1]
    src[:half] = near_ref[...]
    src[half:] = far_ref[...]
    accumulate(count_ref, pick_ref, place_ref, tiles_ref, src, acc, False)
    for y in range(Y):
        for k in range(ZH):
            base = pl.multiple_of((y * ZH + (zh_ref[0] + k) % ZH) * edge, edge)
            out_0[y, k] = acc[pl.ds(base, edge), :wide].astype(BF)
            out_1[y, k] = acc[pl.ds(base, edge), wide:].astype(BF)


def backward_kernel(
    count_ref, pick_ref, place_ref, zh_ref, tiles_ref, ups_0, ups_1, near_ref, far_ref, src, acc
):
    edge = tiles_ref.shape[-1]
    wide = ups_0.shape[-1]
    for y in range(Y):
        for k in range(ZH):
            base = pl.multiple_of((y * ZH + (zh_ref[0] + k) % ZH) * edge, edge)
            src[pl.ds(base, edge), :wide] = ups_0[y, k]
            src[pl.ds(base, edge), wide:] = ups_1[y, k]
    accumulate(count_ref, pick_ref, place_ref, tiles_ref, src, acc, True)
    half = near_ref.shape[0]
    near_ref[...] = acc[:half, :].astype(BF)
    far_ref[...] = acc[half:, :].astype(BF)


def pack_kernel(h, along_y_ref, scaled_ref, out):
    n, wide = scaled_ref.shape[0], out.shape[-1]
    for k in range(ZH):
        summed = along_y_ref[0, k].astype(F32)
        for y in range(1, Y):
            summed += along_y_ref[y, k].astype(F32)
        if k == 0:
            summed += scaled_ref[:, h * wide : (h + 1) * wide].astype(F32)
        out[k * n : (k + 1) * n, :] = summed.astype(BF)


def middle_kernel(
    h, own_ref, back_1_ref, back_2_ref, beside_0, beside_1, beside_2, bias_ref,
    activations_ref, upstream_ref, copies_ref,
):
    shared = (own_ref, back_1_ref, back_2_ref)
    besides = (beside_0, beside_1, beside_2)
    n, wide = activations_ref.shape
    lanes = slice(h * wide, (h + 1) * wide)
    for k in range(ZH):
        gathered = shared[0][k * n : (k + 1) * n, :].astype(F32)
        for j in range(1, ZH):
            first = (k + j) % ZH * n
            gathered += shared[j][first : first + n, :].astype(F32)
        beside = besides[-k % ZH]
        degree = beside[n:, :n].astype(F32)[:1]
        root = lax.rsqrt(jnp.broadcast_to(degree, (wide, n)).T)
        preact = root * gathered + bias_ref[:, lanes]
        sigmoid_value = jax.nn.sigmoid(preact)
        slope_value = sigmoid_value * (1.0 + preact * (1.0 - sigmoid_value))
        cotangents = beside[:n, lanes].astype(F32)
        upstream = (cotangents * slope_value * root).astype(BF)
        if k == 0:
            activations_ref[...] = (preact * sigmoid_value).astype(BF)
            upstream_ref[...] = upstream
        for y in range(Y):
            copies_ref[y, k] = upstream


SMEM = pl.BlockSpec(memory_space=pltpu.SMEM)
VMEM = pl.BlockSpec(memory_space=pltpu.VMEM)


def call(kernel, outs, src_rows, acc_rows, feat, *args):
    return pl.pallas_call(
        kernel,
        out_shape=tuple(jax.ShapeDtypeStruct(s, BF) for s in outs),
        in_specs=[SMEM] * 4 + [VMEM] * (len(args) - 4),
        out_specs=tuple(VMEM for _ in outs),
        scratch_shapes=[pltpu.VMEM((src_rows, feat), BF), pltpu.VMEM((acc_rows, feat), F32)],
        compiler_params=pltpu.CompilerParams(vmem_limit_bytes=24 * 1024 * 1024),
    )(*args)


def call_small(kernel, outs, *args):
    return pl.pallas_call(
        kernel,
        out_shape=tuple(jax.ShapeDtypeStruct(s, BF) for s in outs),
        in_specs=[VMEM] * len(args),
        out_specs=tuple(VMEM for _ in outs),
        compiler_params=pltpu.CompilerParams(vmem_limit_bytes=24 * 1024 * 1024),
    )(*args)


def shift(n, k):
    return [(i, (i + k) % n) for i in range(n)]


def swap(value, axis):
    return lax.all_to_all(value, axis, 0, 0, tiled=True)


def spread(value, axis, size):
    return swap(jnp.broadcast_to(value[None], (size,) + value.shape), axis)


def share(value, axis, size):
    return [value] + [lax.ppermute(value, axis, shift(size, k)) for k in range(1, size)]


def total(value):
    return value.astype(F32).sum(0)


def body(
    features, degrees, weight, bias_term, tile_weights, tile_rows, tile_columns, tile_count, cotangent
):
    tiles = tile_weights[0, 0]
    rows, columns = tile_rows[0, 0], tile_columns[0, 0]
    count = tile_count[0]
    n, feat = features.shape
    wide = feat // 2
    my_zh = lax.axis_index("zh").astype(jnp.int32)[None]
    block_zl, block_x, block_c = columns // (X * C), columns // C % X, columns % C
    other = (block_c != lax.axis_index("c")).astype(jnp.int32)
    column_at = (other * X + block_x) * ZL + block_zl
    sources, targets, chip = C * X * ZL * n, Y * ZH * n, X * ZL * n

    inv_root = lax.rsqrt(degrees.astype(F32))[:, None]
    hidden = jnp.dot(features, weight, preferred_element_type=F32)
    scaled = (hidden * inv_root).astype(BF)

    near = spread(spread(scaled, "zl", ZL), "x", X).reshape(chip, feat)
    far = lax.ppermute(near, "c", shift(C, 1))
    partials = call(
        forward_kernel, [(Y, ZH, n, wide)] * 2, sources, targets, feat,
        count, column_at, rows, my_zh, tiles, near, far,
    )
    degree_rows = jnp.pad(degrees.astype(BF)[None], ((0, 15), (0, feat - n)))
    beside = jnp.concatenate([cotangent, degree_rows], 0)
    partials, beside = lax.optimization_barrier((partials, beside))
    beside = share(beside, "zh", ZH)

    def middle(along_y, h, after):
        along_y, _ = lax.optimization_barrier((along_y, after))
        (mine,) = call_small(functools.partial(pack_kernel, h), [(ZH * n, wide)], along_y, scaled)
        return call_small(
            functools.partial(middle_kernel, h), [(n, wide), (n, wide), (Y, ZH, n, wide)],
            *share(mine, "zh", ZH), *beside, bias_term[None],
        )

    along_y_0 = swap(partials[0], "y")
    along_y_0, partial_1, beside = lax.optimization_barrier((along_y_0, partials[1], beside))
    along_y_1 = swap(partial_1, "y")
    activations_0, upstream_0, along_0 = middle(along_y_0, 0, ())
    activations_1, upstream_1, along_1 = middle(along_y_1, 1, upstream_0)
    ups_0, along_1 = lax.optimization_barrier((swap(along_0, "y"), along_1))
    ups_1 = swap(along_1, "y")

    own, others = call(
        backward_kernel, [(chip, feat)] * 2, targets, sources, feat,
        count, rows, column_at, my_zh, tiles, ups_0, ups_1,
    )
    others = lax.ppermute(others, "c", shift(C, 1))
    back = (own.astype(F32) + others.astype(F32)).astype(BF).reshape(X, ZL * n, feat)
    back = total(swap(back, "x")).astype(BF).reshape(ZL, n, feat)
    own_back = total(swap(back, "zl"))
    upstream = jnp.concatenate([upstream_0, upstream_1], 1)
    grad_hidden = (inv_root * (own_back + upstream.astype(F32))).astype(BF)
    feature_grad = jnp.einsum("nf,gf->ng", grad_hidden, weight, preferred_element_type=F32)
    return jnp.concatenate([activations_0, activations_1], 1), feature_grad.astype(BF)


def solution(mesh):
    fine = Mesh(mesh.devices.reshape(ZL, X, C, Y, ZH), NODE_AXES)
    gr, gc = ("zl", "x", "c"), ("y", "zh")
    nodes = P(NODE_AXES, None)
    return jax.shard_map(
        body,
        mesh=fine,
        in_specs=(
            nodes, P(NODE_AXES), P(), P(), P(gr, gc, None, None, None), P(gr, gc, None), P(gr, gc, None),
            P(gr, gc), nodes,
        ),
        out_specs=(nodes, nodes),
        check_vma=False,
    )
```

```python
import functools

import jax
import jax.numpy as jnp
from jax import lax
from jax.experimental import pallas as pl
from jax.experimental.pallas import tpu as pltpu
from jax.sharding import Mesh
from jax.sharding import PartitionSpec as P

ZL, X, C, Y, ZH = 4, 4, 2, 8, 3
BF, F32 = jnp.bfloat16, jnp.float32
NODE_AXES = ("zl", "x", "c", "y", "zh")
UNROLL = 16


def accumulate(count_ref, pick_ref, place_ref, tiles_ref, src, acc, transposed):
    edge = tiles_ref.shape[-1]
    dims = (((0,), (0,)), ((), ())) if transposed else (((1,), (0,)), ((), ()))
    acc[...] = jnp.zeros_like(acc)

    def step(s, carry):
        for u in range(UNROLL):
            t = s * UNROLL + u
            block = src[pl.ds(pl.multiple_of(pick_ref[t] * edge, edge), edge), :]
            product = lax.dot_general(tiles_ref[t], block, dims, preferred_element_type=F32)
            acc[pl.ds(pl.multiple_of(place_ref[t] * edge, edge), edge), :] += product
        return carry

    lax.fori_loop(0, count_ref[0] // UNROLL, step, 0)


def forward_kernel(
    count_ref, pick_ref, place_ref, tiles_ref, near_ref, far_ref, out_0, out_1, src, acc
):
    half = near_ref.shape[0]
    edge = tiles_ref.shape[-1]
    wide = out_0.shape[-1]
    src[:half] = near_ref[...]
    src[half:] = far_ref[...]
    accumulate(count_ref, pick_ref, place_ref, tiles_ref, src, acc, False)
    for y in range(Y):
        for k in range(ZH):
            base = (y * ZH + k) * edge
            out_0[y, k] = acc[base : base + edge, :wide].astype(BF)
            out_1[y, k] = acc[base : base + edge, wide:].astype(BF)


def backward_kernel(
    count_ref, pick_ref, place_ref, tiles_ref, ups_0, ups_1, near_ref, far_ref, src, acc
):
    edge = tiles_ref.shape[-1]
    wide = ups_0.shape[-1]
    for y in range(Y):
        for k in range(ZH):
            base = (y * ZH + k) * edge
            src[base : base + edge, :wide] = ups_0[y, k]
            src[base : base + edge, wide:] = ups_1[y, k]
    accumulate(count_ref, pick_ref, place_ref, tiles_ref, src, acc, True)
    half = near_ref.shape[0]
    near_ref[...] = acc[:half, :].astype(BF)
    far_ref[...] = acc[half:, :].astype(BF)


def pack_kernel(h, zh_ref, along_y_ref, scaled_ref, out):
    n, wide = scaled_ref.shape[0], out.shape[-1]
    own = scaled_ref[:, h * wide : (h + 1) * wide].astype(F32)
    for k in range(ZH):
        summed = jnp.where(zh_ref[0] == k, own, 0.0)
        for y in range(Y):
            summed += along_y_ref[y, k].astype(F32)
        out[k * n : (k + 1) * n, :] = summed.astype(BF)


def middle_kernel(
    h, zh_ref, shared_ref, beside_ref, bias_ref, activations_ref, upstream_ref, copies_ref
):
    n, wide = activations_ref.shape
    lanes = slice(h * wide, (h + 1) * wide)
    for k in range(ZH):
        gathered = shared_ref[0, k * n : (k + 1) * n, :].astype(F32)
        for j in range(1, ZH):
            gathered += shared_ref[j, k * n : (k + 1) * n, :].astype(F32)
        degree = beside_ref[k, n:, :n].astype(F32)[:1]
        root = lax.rsqrt(jnp.broadcast_to(degree, (wide, n)).T)
        preact = root * gathered + bias_ref[:, lanes]
        sigmoid_value = jax.nn.sigmoid(preact)
        slope_value = sigmoid_value * (1.0 + preact * (1.0 - sigmoid_value))
        cotangents = beside_ref[k, :n, lanes].astype(F32)
        upstream = (cotangents * slope_value * root).astype(BF)
        activations = (preact * sigmoid_value).astype(BF)

        @pl.when(zh_ref[0] == k)
        def _():
            activations_ref[...] = activations
            upstream_ref[...] = upstream

        for y in range(Y):
            copies_ref[y, k] = upstream


SMEM = pl.BlockSpec(memory_space=pltpu.SMEM)
VMEM = pl.BlockSpec(memory_space=pltpu.VMEM)


def call(kernel, outs, src_rows, acc_rows, feat, *args):
    return pl.pallas_call(
        kernel,
        out_shape=tuple(jax.ShapeDtypeStruct(s, BF) for s in outs),
        in_specs=[SMEM] * 3 + [VMEM] * (len(args) - 3),
        out_specs=tuple(VMEM for _ in outs),
        scratch_shapes=[pltpu.VMEM((src_rows, feat), BF), pltpu.VMEM((acc_rows, feat), F32)],
        compiler_params=pltpu.CompilerParams(vmem_limit_bytes=24 * 1024 * 1024),
    )(*args)


def call_small(kernel, outs, *args):
    return pl.pallas_call(
        kernel,
        out_shape=tuple(jax.ShapeDtypeStruct(s, BF) for s in outs),
        in_specs=[SMEM] + [VMEM] * (len(args) - 1),
        out_specs=tuple(VMEM for _ in outs),
        compiler_params=pltpu.CompilerParams(vmem_limit_bytes=24 * 1024 * 1024),
    )(*args)


def shift(n, k):
    return [(i, (i + k) % n) for i in range(n)]


def swap(value, axis):
    return lax.all_to_all(value, axis, 0, 0, tiled=True)


def spread(value, axis, size):
    return swap(jnp.broadcast_to(value[None], (size,) + value.shape), axis)


def total(value):
    return value.astype(F32).sum(0)


def body(
    features, degrees, weight, bias_term, tile_weights, tile_rows, tile_columns, tile_count, cotangent
):
    tiles = tile_weights[0, 0]
    rows, columns = tile_rows[0, 0], tile_columns[0, 0]
    count = tile_count[0]
    n, feat = features.shape
    wide = feat // 2
    my_zh = lax.axis_index("zh").astype(jnp.int32)[None]
    block_zl, block_x, block_c = columns // (X * C), columns // C % X, columns % C
    other = (block_c != lax.axis_index("c")).astype(jnp.int32) * (X * ZL)
    column_at = other + block_x * ZL + block_zl
    sum_at = other + block_zl * X + block_x
    sources, targets, chip = C * X * ZL * n, Y * ZH * n, X * ZL * n

    inv_root = lax.rsqrt(degrees.astype(F32))[:, None]
    hidden = jnp.dot(features, weight, preferred_element_type=F32)
    scaled = (hidden * inv_root).astype(BF)

    near = spread(spread(scaled, "zl", ZL), "x", X).reshape(chip, feat)
    far = lax.ppermute(near, "c", shift(C, 1))
    partials = call(
        forward_kernel, [(Y, ZH, n, wide)] * 2, sources, targets, feat,
        count, column_at, rows, tiles, near, far,
    )
    degree_rows = jnp.pad(degrees.astype(BF)[None], ((0, 15), (0, feat - n)))
    beside = jnp.concatenate([cotangent, degree_rows], 0)
    partials, beside = lax.optimization_barrier((partials, beside))
    beside = lax.all_gather(beside, "zh")

    def middle(along_y, h, after):
        along_y, _ = lax.optimization_barrier((along_y, after))
        (mine,) = call_small(functools.partial(pack_kernel, h), [(ZH * n, wide)], my_zh, along_y, scaled)
        return call_small(
            functools.partial(middle_kernel, h), [(n, wide), (n, wide), (Y, ZH, n, wide)],
            my_zh, lax.all_gather(mine, "zh"), beside, bias_term[None],
        )

    along_y_0 = swap(partials[0], "y")
    along_y_0, partial_1, beside = lax.optimization_barrier((along_y_0, partials[1], beside))
    along_y_1 = swap(partial_1, "y")
    activations_0, upstream_0, along_0 = middle(along_y_0, 0, ())
    activations_1, upstream_1, along_1 = middle(along_y_1, 1, upstream_0)
    ups_0, along_1 = lax.optimization_barrier((swap(along_0, "y"), along_1))
    ups_1 = swap(along_1, "y")

    own, others = call(
        backward_kernel, [(chip, feat)] * 2, targets, sources, feat,
        count, rows, sum_at, tiles, ups_0, ups_1,
    )
    others = lax.ppermute(others, "c", shift(C, 1))
    back = (own.astype(F32) + others.astype(F32)).astype(BF).reshape(ZL * X, n, feat)
    own_back = total(swap(back, ("zl", "x")))
    upstream = jnp.concatenate([upstream_0, upstream_1], 1)
    grad_hidden = (inv_root * (own_back + upstream.astype(F32))).astype(BF)
    feature_grad = jnp.einsum("nf,gf->ng", grad_hidden, weight, preferred_element_type=F32)
    return jnp.concatenate([activations_0, activations_1], 1), feature_grad.astype(BF)


def solution(mesh):
    fine = Mesh(mesh.devices.reshape(ZL, X, C, Y, ZH), NODE_AXES)
    gr, gc = ("zl", "x", "c"), ("y", "zh")
    nodes = P(NODE_AXES, None)
    return jax.shard_map(
        body,
        mesh=fine,
        in_specs=(
            nodes, P(NODE_AXES), P(), P(), P(gr, gc, None, None, None), P(gr, gc, None), P(gr, gc, None),
            P(gr, gc), nodes,
        ),
        out_specs=(nodes, nodes),
        check_vma=False,
    )
```

```python
import functools

import jax
import jax.numpy as jnp
from jax import lax
from jax.experimental import pallas as pl
from jax.experimental.pallas import tpu as pltpu
from jax.sharding import Mesh
from jax.sharding import PartitionSpec as P

ZL, X, C, Y, ZH = 4, 4, 2, 8, 3
BF, F32 = jnp.bfloat16, jnp.float32
NODE_AXES = ("zl", "x", "c", "y", "zh")
UNROLL = 16
PARTS = 4


def fetch(tiles_ref, tiles, sems):
    size = tiles.shape[0] // PARTS
    copies = []
    for part in range(PARTS):
        slots = pl.ds(part * size, size)
        copies.append(pltpu.make_async_copy(tiles_ref.at[slots], tiles.at[slots], sems.at[part]))
        copies[-1].start()
    return copies


def accumulate(count_ref, pick_ref, place_ref, tiles, copies, src, acc, transposed):
    edge = tiles.shape[-1]
    size = tiles.shape[0] // PARTS
    dims = (((0,), (0,)), ((), ())) if transposed else (((1,), (0,)), ((), ()))
    acc[...] = jnp.zeros_like(acc)

    for part in range(PARTS):
        copies[part].wait()

        def step(s, carry, first=part * size):
            for u in range(UNROLL):
                t = first + s * UNROLL + u
                block = src[pl.ds(pl.multiple_of(pick_ref[t] * edge, edge), edge), :]
                product = lax.dot_general(tiles[t], block, dims, preferred_element_type=F32)
                acc[pl.ds(pl.multiple_of(place_ref[t] * edge, edge), edge), :] += product
            return carry

        live = jnp.clip(count_ref[0] - part * size, 0, size)
        lax.fori_loop(0, live // UNROLL, step, 0)


def forward_kernel(
    count_ref, pick_ref, place_ref, tiles_ref, near_ref, far_ref, out_0, out_1, src, acc, tiles, sems
):
    copies = fetch(tiles_ref, tiles, sems)
    half = near_ref.shape[0]
    edge = tiles.shape[-1]
    wide = out_0.shape[-1]
    src[:half] = near_ref[...]
    src[half:] = far_ref[...]
    accumulate(count_ref, pick_ref, place_ref, tiles, copies, src, acc, False)
    for y in range(Y):
        for k in range(ZH):
            base = (y * ZH + k) * edge
            out_0[y, k] = acc[base : base + edge, :wide].astype(BF)
            out_1[y, k] = acc[base : base + edge, wide:].astype(BF)


def backward_kernel(
    count_ref, pick_ref, place_ref, tiles_ref, ups_0, ups_1, near_ref, far_ref, src, acc, tiles, sems
):
    copies = fetch(tiles_ref, tiles, sems)
    edge = tiles.shape[-1]
    wide = ups_0.shape[-1]
    for y in range(Y):
        for k in range(ZH):
            base = (y * ZH + k) * edge
            src[base : base + edge, :wide] = ups_0[y, k]
            src[base : base + edge, wide:] = ups_1[y, k]
    accumulate(count_ref, pick_ref, place_ref, tiles, copies, src, acc, True)
    half = near_ref.shape[0]
    near_ref[...] = acc[:half, :].astype(BF)
    far_ref[...] = acc[half:, :].astype(BF)


def pack_kernel(h, zh_ref, along_y_ref, scaled_ref, out):
    n, wide = scaled_ref.shape[0], out.shape[-1]
    own = scaled_ref[:, h * wide : (h + 1) * wide].astype(F32)
    for k in range(ZH):
        summed = jnp.where(zh_ref[0] == k, own, 0.0)
        for y in range(Y):
            summed += along_y_ref[y, k].astype(F32)
        out[k * n : (k + 1) * n, :] = summed.astype(BF)


def middle_kernel(
    h, zh_ref, shared_ref, beside_ref, bias_ref, activations_ref, upstream_ref, copies_ref
):
    n, wide = activations_ref.shape
    lanes = slice(h * wide, (h + 1) * wide)
    for k in range(ZH):
        gathered = shared_ref[0, k * n : (k + 1) * n, :].astype(F32)
        for j in range(1, ZH):
            gathered += shared_ref[j, k * n : (k + 1) * n, :].astype(F32)
        degree = beside_ref[k, n:, :n].astype(F32)[:1]
        root = lax.rsqrt(jnp.broadcast_to(degree, (wide, n)).T)
        preact = root * gathered + bias_ref[:, lanes]
        sigmoid_value = jax.nn.sigmoid(preact)
        slope_value = sigmoid_value * (1.0 + preact * (1.0 - sigmoid_value))
        cotangents = beside_ref[k, :n, lanes].astype(F32)
        upstream = (cotangents * slope_value * root).astype(BF)
        activations = (preact * sigmoid_value).astype(BF)

        @pl.when(zh_ref[0] == k)
        def _():
            activations_ref[...] = activations
            upstream_ref[...] = upstream

        for y in range(Y):
            copies_ref[y, k] = upstream


SMEM = pl.BlockSpec(memory_space=pltpu.SMEM)
VMEM = pl.BlockSpec(memory_space=pltpu.VMEM)
HBM = pl.BlockSpec(memory_space=pltpu.HBM)


def call(kernel, outs, src_rows, acc_rows, feat, *args):
    tiles = args[3]
    return pl.pallas_call(
        kernel,
        out_shape=tuple(jax.ShapeDtypeStruct(s, BF) for s in outs),
        in_specs=[SMEM] * 3 + [HBM] + [VMEM] * (len(args) - 4),
        out_specs=tuple(VMEM for _ in outs),
        scratch_shapes=[
            pltpu.VMEM((src_rows, feat), BF),
            pltpu.VMEM((acc_rows, feat), F32),
            pltpu.VMEM(tiles.shape, BF),
            pltpu.SemaphoreType.DMA((PARTS,)),
        ],
        compiler_params=pltpu.CompilerParams(vmem_limit_bytes=48 * 1024 * 1024),
    )(*args)


def call_small(kernel, outs, *args):
    return pl.pallas_call(
        kernel,
        out_shape=tuple(jax.ShapeDtypeStruct(s, BF) for s in outs),
        in_specs=[SMEM] + [VMEM] * (len(args) - 1),
        out_specs=tuple(VMEM for _ in outs),
        compiler_params=pltpu.CompilerParams(vmem_limit_bytes=24 * 1024 * 1024),
    )(*args)


def shift(n, k):
    return [(i, (i + k) % n) for i in range(n)]


def swap(value, axis):
    return lax.all_to_all(value, axis, 0, 0, tiled=True)


def spread(value, axis, size):
    return swap(jnp.broadcast_to(value[None], (size,) + value.shape), axis)


def total(value):
    return value.astype(F32).sum(0)


def body(
    features, degrees, weight, bias_term, tile_weights, tile_rows, tile_columns, tile_count, cotangent
):
    tiles = tile_weights[0, 0]
    rows, columns = tile_rows[0, 0], tile_columns[0, 0]
    count = tile_count[0]
    n, feat = features.shape
    wide = feat // 2
    my_zh = lax.axis_index("zh").astype(jnp.int32)[None]
    block_zl, block_x, block_c = columns // (X * C), columns // C % X, columns % C
    other = (block_c != lax.axis_index("c")).astype(jnp.int32) * (X * ZL)
    column_at = other + block_x * ZL + block_zl
    sum_at = other + block_zl * X + block_x
    sources, targets, chip = C * X * ZL * n, Y * ZH * n, X * ZL * n

    inv_root = lax.rsqrt(degrees.astype(F32))[:, None]
    hidden = jnp.dot(features, weight, preferred_element_type=F32)
    scaled = (hidden * inv_root).astype(BF)

    near = spread(spread(scaled, "zl", ZL), "x", X).reshape(chip, feat)
    far = lax.ppermute(near, "c", shift(C, 1))
    partials = call(
        forward_kernel, [(Y, ZH, n, wide)] * 2, sources, targets, feat,
        count, column_at, rows, tiles, near, far,
    )
    degree_rows = jnp.pad(degrees.astype(BF)[None], ((0, 15), (0, feat - n)))
    beside = jnp.concatenate([cotangent, degree_rows], 0)
    partials, beside = lax.optimization_barrier((partials, beside))
    beside = lax.all_gather(beside, "zh")

    def middle(along_y, h, after):
        along_y, _ = lax.optimization_barrier((along_y, after))
        (mine,) = call_small(functools.partial(pack_kernel, h), [(ZH * n, wide)], my_zh, along_y, scaled)
        return call_small(
            functools.partial(middle_kernel, h), [(n, wide), (n, wide), (Y, ZH, n, wide)],
            my_zh, lax.all_gather(mine, "zh"), beside, bias_term[None],
        )

    along_y_0 = swap(partials[0], "y")
    along_y_0, partial_1, beside = lax.optimization_barrier((along_y_0, partials[1], beside))
    along_y_1 = swap(partial_1, "y")
    activations_0, upstream_0, along_0 = middle(along_y_0, 0, ())
    activations_1, upstream_1, along_1 = middle(along_y_1, 1, upstream_0)
    ups_0, along_1 = lax.optimization_barrier((swap(along_0, "y"), along_1))
    ups_1 = swap(along_1, "y")

    own, others = call(
        backward_kernel, [(chip, feat)] * 2, targets, sources, feat,
        count, rows, sum_at, tiles, ups_0, ups_1,
    )
    others = lax.ppermute(others, "c", shift(C, 1))
    back = (own.astype(F32) + others.astype(F32)).astype(BF).reshape(ZL * X, n, feat)
    own_back = total(swap(back, ("zl", "x")))
    upstream = jnp.concatenate([upstream_0, upstream_1], 1)
    grad_hidden = (inv_root * (own_back + upstream.astype(F32))).astype(BF)
    feature_grad = jnp.einsum("nf,gf->ng", grad_hidden, weight, preferred_element_type=F32)
    return jnp.concatenate([activations_0, activations_1], 1), feature_grad.astype(BF)


def solution(mesh):
    fine = Mesh(mesh.devices.reshape(ZL, X, C, Y, ZH), NODE_AXES)
    gr, gc = ("zl", "x", "c"), ("y", "zh")
    nodes = P(NODE_AXES, None)
    return jax.shard_map(
        body,
        mesh=fine,
        in_specs=(
            nodes, P(NODE_AXES), P(), P(), P(gr, gc, None, None, None), P(gr, gc, None), P(gr, gc, None),
            P(gr, gc), nodes,
        ),
        out_specs=(nodes, nodes),
        check_vma=False,
    )
```
